256 devices in a mesh: rows: 64 (over z, y, core), cols: 4 (over x).
Axes of the slice: x: 4, y: 4, z: 8, core: 2. Of those that a mesh axis runs over, the one named last changes fastest.
Arguments:
- train_points: float32 [8, 4, 16384], replicated, may hold values from -1.2 to 1.2
- length_scales: float32 [8], replicated, may hold values from 0.4 to 1.2
- test_points: float32 [8, 4, 2048], P(None, 'cols', 'rows'), may hold values from -1.2 to 1.2
- lower_panel: float32 [4, 512, 16384], P(None, None, 'rows'), as said below
Outputs:
- solved: float32 [4, 8192, 16384], P(None, 'cols', 'rows')
The draws below stay inside these ranges and needn't reach their ends.
Inputs may be any that keep to these rules, and one draw needn't show every extreme that they name: L is lower triangular: lower_panel[0, j, position] is zero where j > position, and its diagonal entries lie in 1 to 2.
All inputs are finite; a program needn't handle non-finite values.
Results may differ from the reference program's by a relative error of at most 0.0001.
Values sent between devices are 32-bit elements; how exact they have to be, the bound alone decides.
A program may use at most 64 MiB of HBM per device.

```python
import math
import jax
import jax.numpy as jnp
from jax import lax

DIM = 8
BLK = 256
STEPS = 2
ROUNDS = 4
SPAN = 16384
GCOLS = 2048
NTEST = 8192
N_COLS = 4


def draw_lower_panel(key, part):
    first, second = jax.random.split(jax.random.fold_in(key, 11))
    shape = (ROUNDS, STEPS * BLK, SPAN)
    noise = jax.random.normal(first, shape, jnp.float32)
    diagonal = jax.random.uniform(second, shape, jnp.float32, 1.0, 2.0)
    rounds = jax.lax.broadcasted_iota(jnp.int32, shape, 0)
    column = jax.lax.broadcasted_iota(jnp.int32, shape, 1)
    position = jax.lax.broadcasted_iota(jnp.int32, shape, 2)
    global_row = rounds * SPAN + position
    same_block = global_row // BLK == column // BLK
    spread = jnp.where(same_block, 0.5 / math.sqrt(BLK), 1.0 / math.sqrt(STEPS * BLK))
    below = noise * spread
    return jnp.where(column < global_row, below, jnp.where(column == global_row, diagonal, jnp.zeros(shape, jnp.float32)))


def level_of(key, extent, pieces, low, largest):
    factor_of, own = 1.0, jax.random.fold_in(key, 6)
    for axis_at, blocks in pieces:
        steps = jnp.exp(jax.random.uniform(jax.random.fold_in(own, axis_at), (blocks,), jnp.float32, low / len(pieces), largest / len(pieces)))
        factor_of = factor_of * jnp.repeat(steps, extent[axis_at] // blocks).reshape([-1 if axis == axis_at else 1 for axis in range(len(extent))])
    return factor_of


def scatter_about(key, dims, width, bound, shards=(), held_as=jnp.bfloat16):
    array = width * jax.random.normal(key, dims, jnp.float32)
    if shards:
        array = array * level_of(key, dims, shards, -0.22, 0.18)
    return jnp.clip(array, -bound, bound).astype(held_as)


def setup_inputs(seed: int = 0) -> dict:
    key_of = jax.random.split(jax.random.key(seed), 5)
    train_points = scatter_about(key_of[0], (DIM, ROUNDS, SPAN), 0.2, 1.2, (), jnp.float32)
    length_scales = jnp.clip(jnp.exp(jax.random.uniform(key_of[1], (DIM,), jnp.float32, math.log(0.4), math.log(1.2))), 0.4, 1.2)
    test_points = scatter_about(key_of[2], (DIM, N_COLS, GCOLS), 0.2, 1.2, ((1, 4), (2, 64)), jnp.float32)
    lower_panel = draw_lower_panel(jax.random.fold_in(key_of[4], 71), 0)
    return {"train_points": train_points, "length_scales": length_scales, "test_points": test_points, "lower_panel": lower_panel}


def kernel_block(train_rows, length_scales, tests):
    total = jnp.zeros((tests.shape[1], train_rows.shape[1]), jnp.float32)
    for feature in range(train_rows.shape[0]):
        differ = (tests[feature][:, None] - train_rows[feature][None, :]) / length_scales[feature]
        total = total + differ * differ
    return jnp.exp(-0.5 * total)

def reference(train_points, length_scales, test_points, lower_panel):
    tests = test_points.reshape(DIM, NTEST)
    head_rows = STEPS * BLK
    head = kernel_block(train_points[:, 0, :head_rows], length_scales, tests)
    slabs = []
    for k in range(STEPS):
        lo = k * BLK
        diag = lower_panel[0, lo:lo + BLK, lo:lo + BLK]
        rhs = head[:, lo:lo + BLK]
        slab = lax.linalg.triangular_solve(diag, rhs, left_side=False, lower=False, transpose_a=False)
        slabs.append(slab)
        head = head - jnp.dot(slab, lower_panel[0, lo:lo + BLK, :head_rows], precision=lax.Precision.HIGHEST)

    def one_round(index):
        train_rows = lax.dynamic_index_in_dim(train_points, index, 1, keepdims=False)
        panel = lax.dynamic_index_in_dim(lower_panel, index, 0, keepdims=False)
        block = kernel_block(train_rows, length_scales, tests)
        for k in range(STEPS):
            lo = k * BLK
            block = block - jnp.dot(slabs[k], panel[lo:lo + BLK, :], precision=lax.Precision.HIGHEST)
        return block
    result = lax.map(one_round, jnp.arange(ROUNDS, dtype=jnp.int32))
    for k in range(STEPS):
        result = result.at[0, :, k * BLK:(k + 1) * BLK].set(slabs[k])
    return result
```

```python
import functools
import math

import jax
import jax.numpy as jnp
from jax import lax
from jax.experimental import pallas as pl
from jax.experimental.pallas import tpu as pltpu
from jax.sharding import PartitionSpec as P

MESH = pl.DeviceIdType.MESH
F32, BF16 = jnp.float32, jnp.bfloat16
LOG2E = math.log2(math.e)

NX, NY, NZ, NC = 4, 4, 8, 2
BLK = 256
HALF = BLK // 2
ROUNDS = 4
DIM = 8
TESTS = 2048
CHUNK = TESTS // NZ
COLS = ROUNDS * BLK
FEAT = 64
PIECE = HALF // NX
TRI = BLK + HALF
SQ = 2 * BLK


def dot(a, b):
    return jnp.dot(a, b, preferred_element_type=F32)


def dot_full(a, b):
    return jnp.dot(a, b, preferred_element_type=F32, precision=lax.Precision.HIGHEST)


def parts3(x):
    h = x.astype(BF16).astype(F32)
    m = (x - h).astype(BF16).astype(F32)
    l = (x - h - m).astype(BF16).astype(F32)
    return h, m, l


def parts2(x):
    h = x.astype(BF16)
    return h, (x - h.astype(F32)).astype(BF16)


def wide(x):
    h, l = parts2(x)
    return jnp.concatenate([h, l, h], axis=1)


def features(points, factor, mirrored):
    n = points.shape[1]
    norm = (-0.5 * LOG2E) * jnp.sum(points * points, axis=0, keepdims=True)
    p1, p2, p3 = parts3(points * factor)
    n1, n2, n3 = parts3(norm)
    row = lax.broadcasted_iota(jnp.int32, (DIM, n), 0)
    base = 3 if mirrored else 0
    own = jnp.where(row == base, n1, jnp.where(row == base + 1, n2, n3))
    mine = (row >= base) & (row < base + 3)
    tail = jnp.where(mine, own, jnp.where(row < 6, 1.0, 0.0))
    order = (p1, p2, p1, p2, p3, p1) if mirrored else (p1, p1, p2, p2, p1, p3)
    return jnp.concatenate(list(order) + [tail, jnp.zeros((DIM, n), F32)], axis=0)


def upper_inverse(u):
    row = lax.broadcasted_iota(jnp.int32, (BLK, BLK), 0)
    col = lax.broadcasted_iota(jnp.int32, (BLK, BLK), 1)
    eye = row == col
    on_diag = jnp.where(eye, u, 0.0)
    d_col = jnp.sum(on_diag, axis=1, keepdims=True)
    d_row = jnp.sum(on_diag, axis=0, keepdims=True)
    strict = jnp.where(col > row, u, 0.0) / d_col
    size = 32
    power = jnp.where(row // size == col // size, -strict, 0.0)
    inverse = jnp.where(eye, 1.0, 0.0) + power
    for _ in range(4):
        power = dot_full(power, power)
        inverse = inverse + dot_full(inverse, power)
    while size < BLK:
        pair = (row // (2 * size) == col // (2 * size)) & (row // size != col // size)
        inverse = inverse - dot_full(dot_full(inverse, jnp.where(pair, strict, 0.0)), inverse)
        size *= 2
    return inverse / d_row


def unpack_tri(packed):
    low = jnp.concatenate([jnp.zeros((HALF, HALF), F32), packed[:, BLK:]], axis=1)
    return jnp.concatenate([packed[:, :BLK], low], axis=0)


def gather_kernel(
    train, scales_hbm, tests_hbm, panel, acc, a0, w0,
    tests, scales, pv, tv, th, tile, slots, group, gathered, feat_t, feat_s, feat_h, a1, w1, p0, p1, p0f,
    vsrc, usrc, gv, gu,
    lsem, sa, ra, sb, rb, sv1, rv1, su1, ru1, sv2, rv2, su2, ru2,
):
    m = lax.axis_index("rows")
    x = lax.axis_index("cols")
    z, y, c = m // 8, (m // 2) % NY, m % 2
    q = m % 8
    is_src = m < 2
    xc = x * 2 + c

    def at(zz, yy, cc, xx):
        return ((zz % NZ) * 8 + (yy % NY) * 2 + cc % 2, xx % NX)

    def in_group(k):
        return (z * 8 + (q + k) % 8, x)

    def in_line(k):
        return at(z + k, y, c, x)

    def in_cross(k):
        o = (xc + k) % 8
        return (z * 8 + y * 2 + o % 2, o // 2)

    loads = [
        pltpu.make_async_copy(panel.at[0], pv.at[0], lsem.at[0]),
        pltpu.make_async_copy(train.at[:, :, pl.ds(pl.multiple_of(m * BLK, BLK), BLK)], tv, lsem.at[1]),
        pltpu.make_async_copy(train.at[:, :, pl.ds(0, 2 * BLK)], th, lsem.at[2]),
        pltpu.make_async_copy(panel.at[pl.ds(1, 3)], pv.at[pl.ds(1, 3)], lsem.at[3]),
        pltpu.make_async_copy(scales_hbm, scales, lsem.at[4]),
    ]
    load_tests = pltpu.make_async_copy(tests_hbm, tests, lsem.at[5])
    load_tests.start()
    for copy in loads:
        copy.start()

    barrier = pltpu.get_barrier_semaphore()
    for k in range(1, 8):
        for who in (in_group(k), in_line(k), in_cross(k)):
            pl.semaphore_signal(barrier, inc=1, device_id=who, device_id_type=MESH)

    @pl.when(jnp.logical_not(is_src))
    def _():
        pl.semaphore_signal(barrier, inc=1, device_id=(c, x), device_id_type=MESH)

    tile[...] = jnp.zeros((DIM, 128), F32)
    load_tests.wait()
    tile[:, pl.ds(0, 32)] = tests[:, 0, :]

    my_rows = pl.ds(pl.multiple_of(x * PIECE, PIECE), PIECE)
    loads[0].wait()

    @pl.when(is_src)
    def _():
        u = pv[0, pl.ds(pl.multiple_of(c * BLK, BLK), BLK), :]
        v = upper_inverse(u)
        vsrc[...] = jnp.concatenate([v[:HALF, :], v[HALF:, HALF:]], axis=1)
        usrc[...] = jnp.concatenate([pv[0, pl.ds(0, HALF), :], pv[0, pl.ds(HALF, HALF), :]], axis=1)

    @pl.when(is_src)
    def _():
        pl.semaphore_wait(barrier, 21 + 31)

    @pl.when(jnp.logical_not(is_src))
    def _():
        pl.semaphore_wait(barrier, 21)

    def remote(src, dst, ssem, rsem, who):
        return pltpu.make_async_remote_copy(
            src_ref=src, dst_ref=dst, send_sem=ssem, recv_sem=rsem, device_id=who, device_id_type=MESH
        )

    def send_a(k):
        return remote(tile, slots.at[q], sa.at[k], ra.at[q], in_group(k))

    def send_b(k):
        return remote(group, gathered.at[z], sb.at[k], rb.at[z], in_line(k))

    def plane(k):
        return at(k // NY, k % NY, c, x)

    def send_v1(k):
        return remote(vsrc.at[my_rows], gv.at[c, my_rows], sv1.at[k], rv1, plane(k))

    def send_u1(k):
        return remote(usrc.at[my_rows], gu.at[my_rows], su1.at[k], ru1, plane(k))

    def send_v2(k):
        return remote(gv.at[c, my_rows], gv.at[c, my_rows], sv2.at[k], rv2.at[c, x], in_cross(k))

    def send_u2(k):
        return remote(gu.at[my_rows], gu.at[my_rows], su2.at[k], ru2.at[x], in_cross(k))

    for k in range(1, 8):
        send_a(k).start()

    @pl.when(is_src & (c == 1))
    def _():
        for k in range(1, 32):
            send_v1(k).start()

    slots[q] = tile[...]
    for k in range(1, 8):
        o = (q + k) % 8
        remote(tile, slots.at[o], sa.at[k], ra.at[o], in_group(k)).wait_recv()
    for h in range(2):
        total = slots[4 * h]
        for j in range(1, 4):
            total = total + pltpu.roll(slots[4 * h + j], 32 * j, 1)
        group[:, pl.ds(128 * h, 128)] = total
    for k in range(1, 8):
        send_b(k).start()
    gathered[z] = group[...]

    @pl.when(is_src & (c == 1))
    def _():
        for k in range(1, 32):
            send_u1(k).start()

    @pl.when(is_src & (c == 0))
    def _():
        for k in range(1, 32):
            send_v1(k).start()

    for copy in loads[1:]:
        copy.wait()
    row8 = lax.broadcasted_iota(jnp.int32, (DIM, 1), 0)
    scale = jnp.zeros((DIM, 1), F32)
    for d in range(DIM):
        scale = jnp.where(row8 == d, scales[d], scale)

    feat_h[...] = features(th[:, 0, :] / scale, LOG2E, True).astype(BF16)
    eye = jnp.where(
        lax.broadcasted_iota(jnp.int32, (BLK, BLK), 0) == lax.broadcasted_iota(jnp.int32, (BLK, BLK), 1), -1.0, 0.0
    )
    for r in range(ROUNDS):
        cols = pl.ds(r * BLK, BLK)
        feat_s[:, cols] = features(tv[:, r, :] / scale, LOG2E, True).astype(BF16)
        lower = pv[r, pl.ds(0, BLK), :]
        upper = pv[r, pl.ds(BLK, BLK), :]
        if r == 0:
            lower = jnp.where(is_src, jnp.where(c == 0, eye, 0.0), lower)
            upper = jnp.where(is_src, jnp.where(c == 1, eye, 0.0), upper)
        p0f[:, cols] = lower
        h, l = parts2(upper)
        p1[pl.ds(0, BLK), cols] = h
        p1[pl.ds(BLK, BLK), cols] = h
        p1[pl.ds(2 * BLK, BLK), cols] = l

    for k in range(NZ):
        o = (z + k) % NZ
        if k:
            remote(group, gathered.at[o], sb.at[k], rb.at[o], in_line(k)).wait_recv()
        feats = features(gathered[o] / scale, 1.0, False)
        feat_t[pl.ds(pl.multiple_of(o * CHUNK, CHUNK), CHUNK), :] = feats.T.astype(BF16)

    def head_chunk(i, _):
        rows = pl.ds(pl.multiple_of(i * CHUNK, CHUNK), CHUNK)
        block = jnp.exp2(dot(feat_t[rows, :], feat_h[...]))
        a0[rows, :] = wide(block[:, :BLK])
        a1[rows, :] = wide(block[:, BLK:])
        return 0

    lax.fori_loop(0, NZ, head_chunk, 0)

    def pass_v():
        @pl.when(jnp.logical_not(is_src))
        def _():
            remote(vsrc.at[my_rows], gv.at[c, my_rows], sv1.at[0], rv1, plane(1)).wait_recv()

        @pl.when(is_src)
        def _():
            gv[c, my_rows, :] = vsrc[my_rows, :]

        for k in range(1, 8):
            send_v2(k).start()

    def pass_u():
        @pl.when(jnp.logical_not(is_src))
        def _():
            remote(usrc.at[my_rows], gu.at[my_rows], su1.at[0], ru1, plane(1)).wait_recv()

        @pl.when(is_src)
        def _():
            gu[my_rows, :] = usrc[my_rows, :]

        for k in range(1, 8):
            send_u2(k).start()

    @pl.when(c == 1)
    def _():
        pass_v()

    keep = jnp.where(is_src, 0.0, 1.0)

    def local_chunk(i, _):
        rows = pl.ds(pl.multiple_of(i * CHUNK, CHUNK), CHUNK)
        block = jnp.exp2(dot(feat_t[rows, :], feat_s[...]))
        acc[rows, pl.ds(0, BLK)] = block[:, :BLK] * keep
        acc[rows, pl.ds(BLK, COLS - BLK)] = block[:, BLK:]
        return 0

    lax.fori_loop(0, NZ, local_chunk, 0)

    @pl.when(c == 1)
    def _():
        pass_u()

    @pl.when(c == 0)
    def _():
        pass_v()

    def wait_v(cc):
        for k in range(NX):
            rows = pl.ds(k * PIECE, PIECE)

            @pl.when(jnp.logical_or(x != k, c != cc))
            def _():
                remote(gv.at[cc, rows], gv.at[cc, rows], sv2.at[0], rv2.at[cc, k], in_cross(1)).wait_recv()

    def wait_u():
        for k in range(NX):
            rows = pl.ds(k * PIECE, PIECE)

            @pl.when(jnp.logical_or(x != k, c != 1))
            def _():
                remote(gu.at[rows], gu.at[rows], su2.at[0], ru2.at[k], in_cross(1)).wait_recv()

    def stack(ref, value):
        h, l = parts2(value)
        ref[pl.ds(0, BLK), :] = h
        ref[pl.ds(BLK, BLK), :] = h
        ref[pl.ds(2 * BLK, BLK), :] = l

    wait_v(1)
    stack(w1, dot(wide(unpack_tri(gv[1])), p1[...]))

    def main_chunk(i, _):
        rows = pl.ds(pl.multiple_of(i * CHUNK, CHUNK), CHUNK)
        acc[rows, :] = acc[rows, :] - dot(a1[rows, :], w1[...])
        return 0

    lax.fori_loop(0, NZ, main_chunk, 0)

    wait_u()
    u01 = jnp.concatenate([gu[:, :BLK], gu[:, BLK:]], axis=0)
    stack(p0, p0f[...] - dot(wide(u01), w1[...]))
    wait_v(0)
    stack(w0, dot(wide(unpack_tri(gv[0])), p0[...]))

    for k in range(1, 8):
        send_a(k).wait_send()
        send_b(k).wait_send()
        send_v2(k).wait_send()

    @pl.when(c == 1)
    def _():
        for k in range(1, 8):
            send_u2(k).wait_send()

    @pl.when(is_src)
    def _():
        for k in range(1, 32):
            send_v1(k).wait_send()

    @pl.when(is_src & (c == 1))
    def _():
        for k in range(1, 32):
            send_u1(k).wait_send()


def finish_kernel(acc, a0, w0, out):
    rows = pl.ds(pl.multiple_of(pl.program_id(0) * CHUNK, CHUNK), CHUNK)
    block = acc[rows, :] - dot(a0[rows, :], w0[...])
    for r in range(ROUNDS):
        out[r] = block[:, r * BLK:(r + 1) * BLK]


def per_device(train_points, length_scales, test_points, lower_panel):
    vmem = pl.BlockSpec(memory_space=pltpu.VMEM)
    dma = pltpu.SemaphoreType.DMA
    acc, a0, w0 = pl.pallas_call(
        gather_kernel,
        out_shape=(
            pltpu.VMEM((TESTS, COLS), F32),
            pltpu.VMEM((TESTS, 3 * BLK), BF16),
            pltpu.VMEM((3 * BLK, COLS), BF16),
        ),
        in_specs=[pl.BlockSpec(memory_space=pltpu.HBM)] * 4,
        out_specs=(vmem, vmem, vmem),
        scratch_shapes=[
            pltpu.VMEM((DIM, 1, 32), F32),
            pltpu.SMEM((DIM,), F32),
            pltpu.VMEM((ROUNDS, 2 * BLK, BLK), F32),
            pltpu.VMEM((DIM, ROUNDS, BLK), F32),
            pltpu.VMEM((DIM, ROUNDS, 2 * BLK), F32),
            pltpu.VMEM((DIM, 128), F32),
            pltpu.VMEM((8, DIM, 128), F32),
            pltpu.VMEM((DIM, CHUNK), F32),
            pltpu.VMEM((NZ, DIM, CHUNK), F32),
            pltpu.VMEM((TESTS, FEAT), BF16),
            pltpu.VMEM((FEAT, COLS), BF16),
            pltpu.VMEM((FEAT, 2 * BLK), BF16),
            pltpu.VMEM((TESTS, 3 * BLK), BF16),
            pltpu.VMEM((3 * BLK, COLS), BF16),
            pltpu.VMEM((3 * BLK, COLS), BF16),
            pltpu.VMEM((3 * BLK, COLS), BF16),
            pltpu.VMEM((BLK, COLS), F32),
            pltpu.VMEM((HALF, TRI), F32),
            pltpu.VMEM((HALF, SQ), F32),
            pltpu.VMEM((2, HALF, TRI), F32),
            pltpu.VMEM((HALF, SQ), F32),
            dma((6,)),
            dma((8,)), dma((8,)), dma((8,)), dma((8,)),
            dma((32,)), dma, dma((32,)), dma,
            dma((8,)), dma((2, NX)), dma((8,)), dma((NX,)),
        ],
        compiler_params=pltpu.CompilerParams(
            collective_id=0, has_side_effects=True, vmem_limit_bytes=32 * 1024 * 1024
        ),
        name="gather_and_half",
    )(*(pltpu.with_memory_space_constraint(a, pltpu.HBM) for a in (train_points, length_scales, test_points, lower_panel)))
    return pl.pallas_call(
        finish_kernel,
        grid=(TESTS // CHUNK,),
        out_shape=jax.ShapeDtypeStruct((ROUNDS, TESTS, BLK), F32),
        in_specs=[vmem, vmem, vmem],
        out_specs=pl.BlockSpec((ROUNDS, CHUNK, BLK), lambda i: (0, i, 0)),
        compiler_params=pltpu.CompilerParams(vmem_limit_bytes=24 * 1024 * 1024),
        name="finish",
    )(acc, a0, w0)


def solution(mesh):
    placed = (P(), P(), P(None, "cols", "rows"), P(None, None, "rows"))
    return jax.shard_map(
        per_device, mesh=mesh, in_specs=placed, out_specs=P(None, "cols", "rows"), check_vma=False
    )
```

```python
import functools
import math

import jax
import jax.numpy as jnp
from jax import lax
from jax.experimental import pallas as pl
from jax.experimental.pallas import tpu as pltpu
from jax.sharding import PartitionSpec as P

MESH = pl.DeviceIdType.MESH
F32, BF16 = jnp.float32, jnp.bfloat16
LOG2E = math.log2(math.e)

NX, NY, NZ, NC = 4, 4, 8, 2
BLK = 256
HALF = BLK // 2
ROUNDS = 4
DIM = 8
TESTS = 2048
CHUNK = TESTS // NZ
TALL = TESTS // 2
COLS = ROUNDS * BLK
FEAT = 64
PIECE = HALF // NX
TRI = BLK + HALF
SQ = 2 * BLK


def dot(a, b):
    return jnp.dot(a, b, preferred_element_type=F32)


def dot_full(a, b):
    return jnp.dot(a, b, preferred_element_type=F32, precision=lax.Precision.HIGHEST)


def parts3(x):
    h = x.astype(BF16).astype(F32)
    m = (x - h).astype(BF16).astype(F32)
    l = (x - h - m).astype(BF16).astype(F32)
    return h, m, l


def parts2(x):
    h = x.astype(BF16)
    return h, (x - h.astype(F32)).astype(BF16)


def wide(x):
    h, l = parts2(x)
    return jnp.concatenate([h, l, h], axis=1)


def features(points, factor, mirrored):
    n = points.shape[1]
    norm = (-0.5 * LOG2E) * jnp.sum(points * points, axis=0, keepdims=True)
    p1, p2, p3 = parts3(points * factor)
    n1, n2, n3 = parts3(norm)
    row = lax.broadcasted_iota(jnp.int32, (DIM, n), 0)
    base = 3 if mirrored else 0
    own = jnp.where(row == base, n1, jnp.where(row == base + 1, n2, n3))
    mine = (row >= base) & (row < base + 3)
    tail = jnp.where(mine, own, jnp.where(row < 6, 1.0, 0.0))
    order = (p1, p2, p1, p2, p3, p1) if mirrored else (p1, p1, p2, p2, p1, p3)
    return jnp.concatenate(list(order) + [tail, jnp.zeros((DIM, n), F32)], axis=0)


def upper_inverse(u):
    row = lax.broadcasted_iota(jnp.int32, (BLK, BLK), 0)
    col = lax.broadcasted_iota(jnp.int32, (BLK, BLK), 1)
    eye = row == col
    on_diag = jnp.where(eye, u, 0.0)
    d_col = jnp.sum(on_diag, axis=1, keepdims=True)
    d_row = jnp.sum(on_diag, axis=0, keepdims=True)
    strict = jnp.where(col > row, u, 0.0) / d_col
    size = 32
    power = jnp.where(row // size == col // size, -strict, 0.0)
    inverse = jnp.where(eye, 1.0, 0.0) + power
    for _ in range(4):
        power = dot_full(power, power)
        inverse = inverse + dot_full(inverse, power)
    while size < BLK:
        pair = (row // (2 * size) == col // (2 * size)) & (row // size != col // size)
        inverse = inverse - dot_full(dot_full(inverse, jnp.where(pair, strict, 0.0)), inverse)
        size *= 2
    return inverse / d_row


def unpack_tri(packed):
    low = jnp.concatenate([jnp.zeros((HALF, HALF), F32), packed[:, BLK:]], axis=1)
    return jnp.concatenate([packed[:, :BLK], low], axis=0)


def gather_kernel(
    train, scales_hbm, tests_hbm, panel, acc, a0, w0,
    tests, scales, pv, tv, th, tile, slots, group, gathered, feat_t, feat_s, feat_h, a1, w1, p0, p1, p0f,
    vsrc, usrc, gv, gu,
    lsem, sa, ra, sb, rb, svy, svz, rv1, suy, suz, ru1, svx, rvx, sux, rux, line_ready,
):
    m = lax.axis_index("rows")
    x = lax.axis_index("cols")
    z, y, c = m // 8, (m // 2) % NY, m % 2
    q = m % 8
    is_src = m < 2
    xc = x * 2 + c

    def at(zz, yy, cc, xx):
        return ((zz % NZ) * 8 + (yy % NY) * 2 + cc % 2, xx % NX)

    def in_group(k):
        return (z * 8 + (q + k) % 8, x)

    def in_line(k):
        return at(z + k, y, c, x)

    def in_cross(k):
        o = (xc + k) % 8
        return (z * 8 + y * 2 + o % 2, o // 2)

    loads = [
        pltpu.make_async_copy(panel.at[0], pv.at[0], lsem.at[0]),
        pltpu.make_async_copy(train.at[:, :, pl.ds(pl.multiple_of(m * BLK, BLK), BLK)], tv, lsem.at[1]),
        pltpu.make_async_copy(train.at[:, :, pl.ds(0, 2 * BLK)], th, lsem.at[2]),
        pltpu.make_async_copy(panel.at[pl.ds(1, 3)], pv.at[pl.ds(1, 3)], lsem.at[3]),
        pltpu.make_async_copy(scales_hbm, scales, lsem.at[4]),
    ]
    load_tests = pltpu.make_async_copy(tests_hbm, tests, lsem.at[5])
    load_tests.start()
    for copy in loads:
        copy.start()

    barrier = pltpu.get_barrier_semaphore()
    is_deputy = (m == 2) | (m == 3)
    for k in range(1, 8):
        line = (z + k) % NZ
        deputy = jnp.where((line == 0) & (y == 0), 1, y)
        for who in (in_group(k), in_cross(k), at(line, deputy, c, x)):
            pl.semaphore_signal(barrier, inc=1, device_id=who, device_id_type=MESH)

    tile[...] = jnp.zeros((DIM, 128), F32)
    load_tests.wait()
    tile[:, pl.ds(0, 32)] = tests[:, 0, :]

    my_rows = pl.ds(pl.multiple_of(x * PIECE, PIECE), PIECE)
    loads[0].wait()

    @pl.when(is_src)
    def _():
        u = pv[0, pl.ds(pl.multiple_of(c * BLK, BLK), BLK), :]
        v = upper_inverse(u)
        vsrc[...] = jnp.concatenate([v[:HALF, :], v[HALF:, HALF:]], axis=1)
        usrc[...] = jnp.concatenate([pv[0, pl.ds(0, HALF), :], pv[0, pl.ds(HALF, HALF), :]], axis=1)

    pl.semaphore_wait(barrier, jnp.where(is_src, 14, jnp.where(is_deputy, 28, 21)))

    @pl.when(is_deputy)
    def _():
        pl.semaphore_signal(line_ready, inc=1, device_id=(c, x), device_id_type=MESH)

    def remote(src, dst, ssem, rsem, who):
        return pltpu.make_async_remote_copy(
            src_ref=src, dst_ref=dst, send_sem=ssem, recv_sem=rsem, device_id=who, device_id_type=MESH
        )

    def send_a(k):
        return remote(tile, slots.at[q], sa.at[k], ra.at[q], in_group(k))

    def send_b(k):
        return remote(group, gathered.at[z], sb.at[k], rb.at[z], in_line(k))

    def send_vy(k):
        return remote(vsrc.at[my_rows], gv.at[c, my_rows], svy.at[k], rv1, at(0, k, c, x))

    def send_uy(k):
        return remote(usrc.at[my_rows], gu.at[my_rows], suy.at[k], ru1, at(0, k, c, x))

    def send_vz(k):
        return remote(gv.at[c, my_rows], gv.at[c, my_rows], svz.at[k], rv1, at(k, y, c, x))

    def send_uz(k):
        return remote(gu.at[my_rows], gu.at[my_rows], suz.at[k], ru1, at(k, y, c, x))

    def send_vx(k):
        return remote(gv.at[c, my_rows], gv.at[c, my_rows], svx.at[k], rvx.at[c, x], in_cross(k))

    def send_ux(k):
        return remote(gu.at[my_rows], gu.at[my_rows], sux.at[k], rux.at[x], in_cross(k))

    def start(send, count):
        for k in range(1, count):
            send(k).start()

    not_src = jnp.logical_not(is_src)
    start(send_a, 8)

    @pl.when(is_src)
    def _():
        start(send_vy, NY)
        gv[c, my_rows, :] = vsrc[my_rows, :]

    @pl.when(is_src & (c == 1))
    def _():
        start(send_uy, NY)
        gu[my_rows, :] = usrc[my_rows, :]

    @pl.when((z == 0) & (c == 1) & not_src)
    def _():
        send_vy(1).wait_recv()
        start(send_vz, NZ)

    @pl.when((z == 0) & (c == 1))
    def _():
        start(send_vx, 8)

    slots[q] = tile[...]
    for k in range(1, 8):
        o = (q + k) % 8
        remote(tile, slots.at[o], sa.at[k], ra.at[o], in_group(k)).wait_recv()
    for h in range(2):
        total = slots[4 * h]
        for j in range(1, 4):
            total = total + pltpu.roll(slots[4 * h + j], 32 * j, 1)
        group[:, pl.ds(128 * h, 128)] = total

    @pl.when(is_src)
    def _():
        pl.semaphore_wait(line_ready, 1)

    @pl.when(is_src & (c == 1))
    def _():
        start(send_vz, NZ)

    start(send_b, 8)
    gathered[z] = group[...]

    @pl.when((z == 0) & (c == 1) & not_src)
    def _():
        send_uy(1).wait_recv()

    @pl.when((z == 0) & (c == 1))
    def _():
        start(send_uz, NZ)
        start(send_ux, 8)

    @pl.when((z == 0) & (c == 0) & not_src)
    def _():
        send_vy(1).wait_recv()

    @pl.when((z == 0) & (c == 0))
    def _():
        start(send_vz, NZ)
        start(send_vx, 8)

    for copy in loads[1:]:
        copy.wait()
    row8 = lax.broadcasted_iota(jnp.int32, (DIM, 1), 0)
    scale = jnp.zeros((DIM, 1), F32)
    for d in range(DIM):
        scale = jnp.where(row8 == d, scales[d], scale)

    feat_h[...] = features(th[:, 0, :] / scale, LOG2E, True).astype(BF16)
    eye = jnp.where(
        lax.broadcasted_iota(jnp.int32, (BLK, BLK), 0) == lax.broadcasted_iota(jnp.int32, (BLK, BLK), 1), -1.0, 0.0
    )
    for r in range(ROUNDS):
        cols = pl.ds(r * BLK, BLK)
        feat_s[:, cols] = features(tv[:, r, :] / scale, LOG2E, True).astype(BF16)
        lower = pv[r, pl.ds(0, BLK), :]
        upper = pv[r, pl.ds(BLK, BLK), :]
        if r == 0:
            lower = jnp.where(is_src, jnp.where(c == 0, eye, 0.0), lower)
            upper = jnp.where(is_src, jnp.where(c == 1, eye, 0.0), upper)
        p0f[:, cols] = lower
        h, l = parts2(upper)
        p1[pl.ds(0, BLK), cols] = h
        p1[pl.ds(BLK, BLK), cols] = h
        p1[pl.ds(2 * BLK, BLK), cols] = l

    @pl.when((z > 0) & (c == 1))
    def _():
        send_vy(1).wait_recv()
        start(send_vx, 8)

    for o in range(NZ):
        @pl.when(z != o)
        def _():
            remote(group, gathered.at[o], sb.at[0], rb.at[o], in_line(1)).wait_recv()

        feat_t[pl.ds(o * CHUNK, CHUNK), :] = features(gathered[o] / scale, 1.0, False).T.astype(BF16)

    def head_chunk(i, _):
        rows = pl.ds(pl.multiple_of(i * CHUNK, CHUNK), CHUNK)
        block = jnp.exp2(dot(feat_t[rows, :], feat_h[...]))
        a0[rows, :] = wide(block[:, :BLK])
        a1[rows, :] = wide(block[:, BLK:])
        return 0

    lax.fori_loop(0, NZ, head_chunk, 0)

    @pl.when((z > 0) & (c == 1))
    def _():
        send_uy(1).wait_recv()
        start(send_ux, 8)

    @pl.when((z > 0) & (c == 0))
    def _():
        send_vy(1).wait_recv()
        start(send_vx, 8)

    keep = jnp.where(is_src, 0.0, 1.0)

    def local_chunk(i, _):
        rows = pl.ds(pl.multiple_of(i * CHUNK, CHUNK), CHUNK)
        block = jnp.exp2(dot(feat_t[rows, :], feat_s[...]))
        acc[rows, pl.ds(0, BLK)] = block[:, :BLK] * keep
        acc[rows, pl.ds(BLK, COLS - BLK)] = block[:, BLK:]
        return 0

    lax.fori_loop(0, NZ, local_chunk, 0)

    def wait_v(cc):
        for k in range(NX):
            rows = pl.ds(k * PIECE, PIECE)

            @pl.when(jnp.logical_or(x != k, c != cc))
            def _():
                remote(gv.at[cc, rows], gv.at[cc, rows], svx.at[0], rvx.at[cc, k], in_cross(1)).wait_recv()

    def wait_u():
        for k in range(NX):
            rows = pl.ds(k * PIECE, PIECE)

            @pl.when(jnp.logical_or(x != k, c != 1))
            def _():
                remote(gu.at[rows], gu.at[rows], sux.at[0], rux.at[k], in_cross(1)).wait_recv()

    def stack(ref, value):
        h, l = parts2(value)
        ref[pl.ds(0, BLK), :] = h
        ref[pl.ds(BLK, BLK), :] = h
        ref[pl.ds(2 * BLK, BLK), :] = l

    wait_v(1)
    stack(w1, dot(wide(unpack_tri(gv[1])), p1[...]))

    def main_chunk(i, _):
        rows = pl.ds(pl.multiple_of((i % 2) * TALL, TALL), TALL)
        cols = pl.ds(pl.multiple_of((i // 2) * BLK, BLK), BLK)
        acc[rows, cols] = acc[rows, cols] - dot(a1[rows, :], w1[:, cols])
        return 0

    lax.fori_loop(0, 2 * ROUNDS, main_chunk, 0)

    wait_u()
    u01 = jnp.concatenate([gu[:, :BLK], gu[:, BLK:]], axis=0)
    stack(p0, p0f[...] - dot(wide(u01), w1[...]))
    wait_v(0)
    stack(w0, dot(wide(unpack_tri(gv[0])), p0[...]))

    def sent(send, count):
        for k in range(1, count):
            send(k).wait_send()

    for send in (send_a, send_b, send_vx):
        sent(send, 8)

    @pl.when(z == 0)
    def _():
        sent(send_vz, NZ)

    @pl.when(c == 1)
    def _():
        sent(send_ux, 8)

    @pl.when((z == 0) & (c == 1))
    def _():
        sent(send_uz, NZ)

    @pl.when(is_src)
    def _():
        sent(send_vy, NY)

    @pl.when(is_src & (c == 1))
    def _():
        sent(send_uy, NY)


def finish_kernel(acc, a0, w0, out):
    rows = pl.ds(pl.multiple_of(pl.program_id(0) * (TESTS // 4), TESTS // 4), TESTS // 4)
    block = acc[rows, :] - dot(a0[rows, :], w0[...])
    for r in range(ROUNDS):
        out[r] = block[:, r * BLK:(r + 1) * BLK]


def per_device(train_points, length_scales, test_points, lower_panel):
    vmem = pl.BlockSpec(memory_space=pltpu.VMEM)
    dma = pltpu.SemaphoreType.DMA
    acc, a0, w0 = pl.pallas_call(
        gather_kernel,
        out_shape=(
            pltpu.VMEM((TESTS, COLS), F32),
            pltpu.VMEM((TESTS, 3 * BLK), BF16),
            pltpu.VMEM((3 * BLK, COLS), BF16),
        ),
        in_specs=[pl.BlockSpec(memory_space=pltpu.HBM)] * 4,
        out_specs=(vmem, vmem, vmem),
        scratch_shapes=[
            pltpu.VMEM((DIM, 1, 32), F32),
            pltpu.SMEM((DIM,), F32),
            pltpu.VMEM((ROUNDS, 2 * BLK, BLK), F32),
            pltpu.VMEM((DIM, ROUNDS, BLK), F32),
            pltpu.VMEM((DIM, ROUNDS, 2 * BLK), F32),
            pltpu.VMEM((DIM, 128), F32),
            pltpu.VMEM((8, DIM, 128), F32),
            pltpu.VMEM((DIM, CHUNK), F32),
            pltpu.VMEM((NZ, DIM, CHUNK), F32),
            pltpu.VMEM((TESTS, FEAT), BF16),
            pltpu.VMEM((FEAT, COLS), BF16),
            pltpu.VMEM((FEAT, 2 * BLK), BF16),
            pltpu.VMEM((TESTS, 3 * BLK), BF16),
            pltpu.VMEM((3 * BLK, COLS), BF16),
            pltpu.VMEM((3 * BLK, COLS), BF16),
            pltpu.VMEM((3 * BLK, COLS), BF16),
            pltpu.VMEM((BLK, COLS), F32),
            pltpu.VMEM((HALF, TRI), F32),
            pltpu.VMEM((HALF, SQ), F32),
            pltpu.VMEM((2, HALF, TRI), F32),
            pltpu.VMEM((HALF, SQ), F32),
            dma((6,)),
            dma((8,)), dma((8,)), dma((8,)), dma((8,)),
            dma((NY,)), dma((NZ,)), dma, dma((NY,)), dma((NZ,)), dma,
            dma((8,)), dma((2, NX)), dma((8,)), dma((NX,)),
            pltpu.SemaphoreType.REGULAR,
        ],
        compiler_params=pltpu.CompilerParams(
            collective_id=0, has_side_effects=True, vmem_limit_bytes=32 * 1024 * 1024
        ),
        name="gather_and_half",
    )(*(pltpu.with_memory_space_constraint(a, pltpu.HBM) for a in (train_points, length_scales, test_points, lower_panel)))
    return pl.pallas_call(
        finish_kernel,
        grid=(4,),
        out_shape=jax.ShapeDtypeStruct((ROUNDS, TESTS, BLK), F32),
        in_specs=[vmem, vmem, vmem],
        out_specs=pl.BlockSpec((ROUNDS, TESTS // 4, BLK), lambda i: (0, i, 0)),
        compiler_params=pltpu.CompilerParams(vmem_limit_bytes=24 * 1024 * 1024),
        name="finish",
    )(acc, a0, w0)


def solution(mesh):
    placed = (P(), P(), P(None, "cols", "rows"), P(None, None, "rows"))
    return jax.shard_map(
        per_device, mesh=mesh, in_specs=placed, out_specs=P(None, "cols", "rows"), check_vma=False
    )
```

```python
import functools
import math

import jax
import jax.numpy as jnp
from jax import lax
from jax.experimental import pallas as pl
from jax.experimental.pallas import tpu as pltpu
from jax.sharding import PartitionSpec as P

MESH = pl.DeviceIdType.MESH
F32, BF16 = jnp.float32, jnp.bfloat16
LOG2E = math.log2(math.e)

NX, NY, NZ, NC = 4, 4, 8, 2
BLK = 256
HALF = BLK // 2
ROUNDS = 4
DIM = 8
TESTS = 2048
CHUNK = TESTS // NZ
TALL = TESTS // 2
TILE = TESTS // 8
COLS = ROUNDS * BLK
FEAT = 64
PIECE = HALF // NX
TRI = BLK + HALF
SQ = 2 * BLK


def dot(a, b):
    return jnp.dot(a, b, preferred_element_type=F32)


def dot_full(a, b):
    return jnp.dot(a, b, preferred_element_type=F32, precision=lax.Precision.HIGHEST)


def parts3(x):
    h = x.astype(BF16).astype(F32)
    m = (x - h).astype(BF16).astype(F32)
    l = (x - h - m).astype(BF16).astype(F32)
    return h, m, l


def parts2(x):
    h = x.astype(BF16)
    return h, (x - h.astype(F32)).astype(BF16)


def wide(x):
    h, l = parts2(x)
    return jnp.concatenate([h, l, h], axis=1)


def features(points, factor, mirrored):
    n = points.shape[1]
    norm = (-0.5 * LOG2E) * jnp.sum(points * points, axis=0, keepdims=True)
    p1, p2, p3 = parts3(points * factor)
    n1, n2, n3 = parts3(norm)
    row = lax.broadcasted_iota(jnp.int32, (DIM, n), 0)
    base = 3 if mirrored else 0
    own = jnp.where(row == base, n1, jnp.where(row == base + 1, n2, n3))
    mine = (row >= base) & (row < base + 3)
    tail = jnp.where(mine, own, jnp.where(row < 6, 1.0, 0.0))
    order = (p1, p2, p1, p2, p3, p1) if mirrored else (p1, p1, p2, p2, p1, p3)
    return jnp.concatenate(list(order) + [tail, jnp.zeros((DIM, n), F32)], axis=0)


def upper_inverse(u):
    row = lax.broadcasted_iota(jnp.int32, (BLK, BLK), 0)
    col = lax.broadcasted_iota(jnp.int32, (BLK, BLK), 1)
    on_diag = jnp.where(row == col, u, 0.0)
    d_col = jnp.sum(on_diag, axis=1, keepdims=True)
    d_row = jnp.sum(on_diag, axis=0, keepdims=True)
    strict = jnp.where(col > row, u, 0.0) / d_col
    row, col = row[:HALF, :HALF], col[:HALF, :HALF]
    blocks = [strict[:HALF, :HALF], strict[HALF:, HALF:]]
    size = 32
    powers = [jnp.where(row // size == col // size, -n, 0.0) for n in blocks]
    inverses = [jnp.where(row == col, 1.0, 0.0) + p for p in powers]
    for _ in range(4):
        powers = [dot_full(p, p) for p in powers]
        inverses = [v + dot_full(v, p) for v, p in zip(inverses, powers)]
    while size < HALF:
        pair = (row // (2 * size) == col // (2 * size)) & (row // size != col // size)
        halves = [dot_full(v, jnp.where(pair, n, 0.0)) for v, n in zip(inverses, blocks)]
        inverses = [v - dot_full(h, v) for v, h in zip(inverses, halves)]
        size *= 2
    corner = -dot_full(dot_full(inverses[0], strict[:HALF, HALF:]), inverses[1])
    top = jnp.concatenate([inverses[0], corner], axis=1) / d_row
    return jnp.concatenate([top, inverses[1] / d_row[:, HALF:]], axis=1)


def unpack_tri(packed):
    low = jnp.concatenate([jnp.zeros((HALF, HALF), F32), packed[:, BLK:]], axis=1)
    return jnp.concatenate([packed[:, :BLK], low], axis=0)


def gather_kernel(
    train, scales_hbm, tests_hbm, panel, acc, a0, w0,
    tests, scales, pv, tv, th, tile, slots, group, gathered, feat_t, feat_s, feat_h, a1, w1, p0, p1, p0f,
    vsrc, usrc, gv, gu,
    lsem, sa, ra, sb, rb, svy, svz, rv1, suy, suz, ru1, svx, rvx, sux, rux, line_ready,
):
    m = lax.axis_index("rows")
    x = lax.axis_index("cols")
    z, y, c = m // 8, (m // 2) % NY, m % 2
    q = m % 8
    is_src = m < 2
    xc = x * 2 + c

    def at(zz, yy, cc, xx):
        return ((zz % NZ) * 8 + (yy % NY) * 2 + cc % 2, xx % NX)

    def in_group(k):
        return (z * 8 + (q + k) % 8, x)

    def in_line(k):
        return at(z + k, y, c, x)

    def in_cross(k):
        o = (xc + k) % 8
        return (z * 8 + y * 2 + o % 2, o // 2)

    loads = [
        pltpu.make_async_copy(panel.at[0], pv.at[0], lsem.at[0]),
        pltpu.make_async_copy(train.at[:, :, pl.ds(pl.multiple_of(m * BLK, BLK), BLK)], tv, lsem.at[1]),
        pltpu.make_async_copy(train.at[:, :, pl.ds(0, 2 * BLK)], th, lsem.at[2]),
        pltpu.make_async_copy(panel.at[pl.ds(1, 3)], pv.at[pl.ds(1, 3)], lsem.at[3]),
        pltpu.make_async_copy(scales_hbm, scales, lsem.at[4]),
    ]
    load_tests = pltpu.make_async_copy(tests_hbm, tests, lsem.at[5])
    load_tests.start()
    for copy in loads:
        copy.start()

    barrier = pltpu.get_barrier_semaphore()
    is_deputy = (m == 2) | (m == 3)
    for k in range(1, 8):
        line = (z + k) % NZ
        deputy = jnp.where((line == 0) & (y == 0), 1, y)
        for who in (in_group(k), in_cross(k), at(line, deputy, c, x)):
            pl.semaphore_signal(barrier, inc=1, device_id=who, device_id_type=MESH)

    tile[...] = jnp.zeros((DIM, 128), F32)
    load_tests.wait()
    tile[:, pl.ds(0, 32)] = tests[:, 0, :]

    my_rows = pl.ds(pl.multiple_of(x * PIECE, PIECE), PIECE)
    loads[0].wait()

    @pl.when(is_src)
    def _():
        vsrc[...] = upper_inverse(pv[0, pl.ds(pl.multiple_of(c * BLK, BLK), BLK), :])
        usrc[...] = jnp.concatenate([pv[0, pl.ds(0, HALF), :], pv[0, pl.ds(HALF, HALF), :]], axis=1)

    pl.semaphore_wait(barrier, jnp.where(is_src, 14, jnp.where(is_deputy, 28, 21)))

    @pl.when(is_deputy)
    def _():
        pl.semaphore_signal(line_ready, inc=1, device_id=(c, x), device_id_type=MESH)

    def remote(src, dst, ssem, rsem, who):
        return pltpu.make_async_remote_copy(
            src_ref=src, dst_ref=dst, send_sem=ssem, recv_sem=rsem, device_id=who, device_id_type=MESH
        )

    def send_a(k):
        return remote(tile, slots.at[q], sa.at[k], ra.at[q], in_group(k))

    def send_b(k):
        return remote(group, gathered.at[z], sb.at[k], rb.at[z], in_line(k))

    def send_vy(k):
        return remote(vsrc.at[my_rows], gv.at[c, my_rows], svy.at[k], rv1, at(0, k, c, x))

    def send_uy(k):
        return remote(usrc.at[my_rows], gu.at[my_rows], suy.at[k], ru1, at(0, k, c, x))

    def send_vz(k):
        return remote(gv.at[c, my_rows], gv.at[c, my_rows], svz.at[k], rv1, at(k, y, c, x))

    def send_uz(k):
        return remote(gu.at[my_rows], gu.at[my_rows], suz.at[k], ru1, at(k, y, c, x))

    def send_vx(k):
        return remote(gv.at[c, my_rows], gv.at[c, my_rows], svx.at[k], rvx.at[c, x], in_cross(k))

    def send_ux(k):
        return remote(gu.at[my_rows], gu.at[my_rows], sux.at[k], rux.at[x], in_cross(k))

    def start(send, count):
        for k in range(1, count):
            send(k).start()

    not_src = jnp.logical_not(is_src)
    start(send_a, 8)

    @pl.when(is_src)
    def _():
        start(send_vy, NY)
        gv[c, my_rows, :] = vsrc[my_rows, :]

    @pl.when(is_src & (c == 1))
    def _():
        start(send_uy, NY)
        gu[my_rows, :] = usrc[my_rows, :]

    @pl.when(is_src)
    def _():
        pl.semaphore_wait(line_ready, 1)

    @pl.when((z == 0) & (c == 1) & not_src)
    def _():
        send_vy(1).wait_recv()

    @pl.when((z == 0) & (c == 1))
    def _():
        start(send_vz, NZ)
        start(send_vx, 8)

    @pl.when((z == 0) & (c == 1) & not_src)
    def _():
        send_uy(1).wait_recv()

    @pl.when((z == 0) & (c == 1))
    def _():
        start(send_uz, NZ)
        start(send_ux, 8)

    slots[q] = tile[...]
    for k in range(1, 8):
        o = (q + k) % 8
        remote(tile, slots.at[o], sa.at[k], ra.at[o], in_group(k)).wait_recv()
    for h in range(2):
        total = slots[4 * h]
        for j in range(1, 4):
            total = total + pltpu.roll(slots[4 * h + j], 32 * j, 1)
        group[:, pl.ds(128 * h, 128)] = total

    start(send_b, 8)
    gathered[z] = group[...]

    @pl.when((z == 0) & (c == 0) & not_src)
    def _():
        send_vy(1).wait_recv()

    @pl.when((z == 0) & (c == 0))
    def _():
        start(send_vz, NZ)
        start(send_vx, 8)

    for copy in loads[1:]:
        copy.wait()
    row8 = lax.broadcasted_iota(jnp.int32, (DIM, 1), 0)
    scale = jnp.zeros((DIM, 1), F32)
    for d in range(DIM):
        scale = jnp.where(row8 == d, scales[d], scale)

    feat_h[...] = features(th[:, 0, :] / scale, LOG2E, True).astype(BF16)
    eye = jnp.where(
        lax.broadcasted_iota(jnp.int32, (BLK, BLK), 0) == lax.broadcasted_iota(jnp.int32, (BLK, BLK), 1), -1.0, 0.0
    )
    for r in range(ROUNDS):
        cols = pl.ds(r * BLK, BLK)
        feat_s[:, cols] = features(tv[:, r, :] / scale, LOG2E, True).astype(BF16)
        lower = pv[r, pl.ds(0, BLK), :]
        upper = pv[r, pl.ds(BLK, BLK), :]
        if r == 0:
            lower = jnp.where(is_src, jnp.where(c == 0, eye, 0.0), lower)
            upper = jnp.where(is_src, jnp.where(c == 1, eye, 0.0), upper)
        p0f[:, cols] = lower
        h, l = parts2(upper)
        p1[pl.ds(0, BLK), cols] = h
        p1[pl.ds(BLK, BLK), cols] = h
        p1[pl.ds(2 * BLK, BLK), cols] = l

    def wait_v(cc):
        for k in range(NX):
            rows = pl.ds(k * PIECE, PIECE)

            @pl.when(jnp.logical_or(x != k, c != cc))
            def _():
                remote(gv.at[cc, rows], gv.at[cc, rows], svx.at[0], rvx.at[cc, k], in_cross(1)).wait_recv()

    def wait_u():
        for k in range(NX):
            rows = pl.ds(k * PIECE, PIECE)

            @pl.when(jnp.logical_or(x != k, c != 1))
            def _():
                remote(gu.at[rows], gu.at[rows], sux.at[0], rux.at[k], in_cross(1)).wait_recv()

    def stack(ref, value):
        h, l = parts2(value)
        ref[pl.ds(0, BLK), :] = h
        ref[pl.ds(BLK, BLK), :] = h
        ref[pl.ds(2 * BLK, BLK), :] = l

    def first_weights():
        wait_v(1)
        stack(w1, dot(wide(unpack_tri(gv[1])), p1[...]))

    def second_weights():
        wait_u()
        u01 = jnp.concatenate([gu[:, :BLK], gu[:, BLK:]], axis=0)
        stack(p0, p0f[...] - dot(wide(u01), w1[...]))
        wait_v(0)
        stack(w0, dot(wide(unpack_tri(gv[0])), p0[...]))

    keep = jnp.where(is_src, 0.0, 1.0)

    def covariance(half):
        for o in range(half * NZ // 2, (half + 1) * NZ // 2):
            @pl.when(z != o)
            def _():
                remote(group, gathered.at[o], sb.at[0], rb.at[o], in_line(1)).wait_recv()

            feat_t[pl.ds(o * CHUNK, CHUNK), :] = features(gathered[o] / scale, 1.0, False).T.astype(BF16)
        rows = pl.ds(half * TALL, TALL)
        block = jnp.exp2(dot(feat_t[rows, :], feat_h[...]))
        a0[rows, :] = wide(block[:, :BLK])
        a1[rows, :] = wide(block[:, BLK:])
        block = jnp.exp2(dot(feat_t[rows, :], feat_s[...]))
        acc[rows, pl.ds(0, BLK)] = block[:, :BLK] * keep
        acc[rows, pl.ds(BLK, COLS - BLK)] = block[:, BLK:]

    def main_chunk(i, _):
        rows = pl.ds(pl.multiple_of(i * TALL, TALL), TALL)
        acc[rows, :] = acc[rows, :] - dot(a1[rows, :], w1[...])
        return 0

    @pl.when(z > 0)
    def _():
        send_vy(1).wait_recv()
        start(send_vx, 8)

    @pl.when((z > 0) & (c == 1))
    def _():
        send_uy(1).wait_recv()
        start(send_ux, 8)

    covariance(0)

    covariance(1)

    first_weights()

    lax.fori_loop(0, TESTS // TALL, main_chunk, 0)

    second_weights()

    def sent(send, count):
        for k in range(1, count):
            send(k).wait_send()

    for send in (send_a, send_b, send_vx):
        sent(send, 8)

    @pl.when(z == 0)
    def _():
        sent(send_vz, NZ)

    @pl.when(c == 1)
    def _():
        sent(send_ux, 8)

    @pl.when((z == 0) & (c == 1))
    def _():
        sent(send_uz, NZ)

    @pl.when(is_src)
    def _():
        sent(send_vy, NY)

    @pl.when(is_src & (c == 1))
    def _():
        sent(send_uy, NY)


def finish_kernel(acc, a0, w0, out, done, sem):
    copies = []
    for i in range(TESTS // TILE):
        rows = pl.ds(i * TILE, TILE)
        block = acc[rows, :] - dot(a0[rows, :], w0[...])
        for r in range(ROUNDS):
            done[r, rows, :] = block[:, r * BLK:(r + 1) * BLK]
            copies.append(pltpu.make_async_copy(done.at[r, rows], out.at[r, rows], sem.at[i * ROUNDS + r]))
            copies[-1].start()
    for copy in copies:
        copy.wait()


def per_device(train_points, length_scales, test_points, lower_panel):
    vmem = pl.BlockSpec(memory_space=pltpu.VMEM)
    dma = pltpu.SemaphoreType.DMA
    acc, a0, w0 = pl.pallas_call(
        gather_kernel,
        out_shape=(
            pltpu.VMEM((TESTS, COLS), F32),
            pltpu.VMEM((TESTS, 3 * BLK), BF16),
            pltpu.VMEM((3 * BLK, COLS), BF16),
        ),
        in_specs=[pl.BlockSpec(memory_space=pltpu.HBM)] * 4,
        out_specs=(vmem, vmem, vmem),
        scratch_shapes=[
            pltpu.VMEM((DIM, 1, 32), F32),
            pltpu.SMEM((DIM,), F32),
            pltpu.VMEM((ROUNDS, 2 * BLK, BLK), F32),
            pltpu.VMEM((DIM, ROUNDS, BLK), F32),
            pltpu.VMEM((DIM, ROUNDS, 2 * BLK), F32),
            pltpu.VMEM((DIM, 128), F32),
            pltpu.VMEM((8, DIM, 128), F32),
            pltpu.VMEM((DIM, CHUNK), F32),
            pltpu.VMEM((NZ, DIM, CHUNK), F32),
            pltpu.VMEM((TESTS, FEAT), BF16),
            pltpu.VMEM((FEAT, COLS), BF16),
            pltpu.VMEM((FEAT, 2 * BLK), BF16),
            pltpu.VMEM((TESTS, 3 * BLK), BF16),
            pltpu.VMEM((3 * BLK, COLS), BF16),
            pltpu.VMEM((3 * BLK, COLS), BF16),
            pltpu.VMEM((3 * BLK, COLS), BF16),
            pltpu.VMEM((BLK, COLS), F32),
            pltpu.VMEM((HALF, TRI), F32),
            pltpu.VMEM((HALF, SQ), F32),
            pltpu.VMEM((2, HALF, TRI), F32),
            pltpu.VMEM((HALF, SQ), F32),
            dma((6,)),
            dma((8,)), dma((8,)), dma((8,)), dma((8,)),
            dma((NY,)), dma((NZ,)), dma, dma((NY,)), dma((NZ,)), dma,
            dma((8,)), dma((2, NX)), dma((8,)), dma((NX,)),
            pltpu.SemaphoreType.REGULAR,
        ],
        compiler_params=pltpu.CompilerParams(
            collective_id=0, has_side_effects=True, vmem_limit_bytes=32 * 1024 * 1024
        ),
        name="gather_and_half",
    )(*(pltpu.with_memory_space_constraint(a, pltpu.HBM) for a in (train_points, length_scales, test_points, lower_panel)))
    return pl.pallas_call(
        finish_kernel,
        out_shape=jax.ShapeDtypeStruct((ROUNDS, TESTS, BLK), F32),
        in_specs=[vmem, vmem, vmem],
        out_specs=pl.BlockSpec(memory_space=pltpu.HBM),
        scratch_shapes=[pltpu.VMEM((ROUNDS, TESTS, BLK), F32), dma((ROUNDS * TESTS // TILE,))],
        compiler_params=pltpu.CompilerParams(vmem_limit_bytes=24 * 1024 * 1024),
        name="finish",
    )(acc, a0, w0)


def solution(mesh):
    placed = (P(), P(), P(None, "cols", "rows"), P(None, None, "rows"))
    return jax.shard_map(
        per_device, mesh=mesh, in_specs=placed, out_specs=P(None, "cols", "rows"), check_vma=False
    )
```

```python
import functools
import math

import jax
import jax.numpy as jnp
from jax import lax
from jax.experimental import pallas as pl
from jax.experimental.pallas import tpu as pltpu
from jax.sharding import PartitionSpec as P

MESH = pl.DeviceIdType.MESH
F32, BF16 = jnp.float32, jnp.bfloat16
LOG2E = math.log2(math.e)

NX, NY, NZ, NC = 4, 4, 8, 2
BLK = 256
HALF = BLK // 2
ROUNDS = 4
DIM = 8
TESTS = 2048
CHUNK = TESTS // NZ
TALL = TESTS // 2
SIZES = (1, 1, 2, 2, 1, 1)
ARRIVAL = (0, 1, 7, 2, 6, 3, 5, 4)
COLS = ROUNDS * BLK
FEAT = 64
PIECE = HALF // NX
TRI = BLK + HALF
SQ = 2 * BLK


def dot(a, b):
    return jnp.dot(a, b, preferred_element_type=F32)


def dot_full(a, b):
    return jnp.dot(a, b, preferred_element_type=F32, precision=lax.Precision.HIGHEST)


def parts3(x):
    h = x.astype(BF16).astype(F32)
    m = (x - h).astype(BF16).astype(F32)
    l = (x - h - m).astype(BF16).astype(F32)
    return h, m, l


def parts2(x):
    h = x.astype(BF16)
    return h, (x - h.astype(F32)).astype(BF16)


def wide(x):
    h, l = parts2(x)
    return jnp.concatenate([h, l, h], axis=1)


def features(points, factor, mirrored):
    n = points.shape[1]
    norm = (-0.5 * LOG2E) * jnp.sum(points * points, axis=0, keepdims=True)
    p1, p2, p3 = parts3(points * factor)
    n1, n2, n3 = parts3(norm)
    row = lax.broadcasted_iota(jnp.int32, (DIM, n), 0)
    base = 3 if mirrored else 0
    own = jnp.where(row == base, n1, jnp.where(row == base + 1, n2, n3))
    mine = (row >= base) & (row < base + 3)
    tail = jnp.where(mine, own, jnp.where(row < 6, 1.0, 0.0))
    order = (p1, p2, p1, p2, p3, p1) if mirrored else (p1, p1, p2, p2, p1, p3)
    return jnp.concatenate(list(order) + [tail, jnp.zeros((DIM, n), F32)], axis=0)


def upper_inverse(u):
    row = lax.broadcasted_iota(jnp.int32, (BLK, BLK), 0)
    col = lax.broadcasted_iota(jnp.int32, (BLK, BLK), 1)
    on_diag = jnp.where(row == col, u, 0.0)
    d_col = jnp.sum(on_diag, axis=1, keepdims=True)
    d_row = jnp.sum(on_diag, axis=0, keepdims=True)
    strict = jnp.where(col > row, u, 0.0) / d_col
    row, col = row[:HALF, :HALF], col[:HALF, :HALF]
    blocks = [strict[:HALF, :HALF], strict[HALF:, HALF:]]
    size = 32
    powers = [jnp.where(row // size == col // size, -n, 0.0) for n in blocks]
    inverses = [jnp.where(row == col, 1.0, 0.0) + p for p in powers]
    for _ in range(4):
        powers = [dot_full(p, p) for p in powers]
        inverses = [v + dot_full(v, p) for v, p in zip(inverses, powers)]
    while size < HALF:
        pair = (row // (2 * size) == col // (2 * size)) & (row // size != col // size)
        halves = [dot_full(v, jnp.where(pair, n, 0.0)) for v, n in zip(inverses, blocks)]
        inverses = [v - dot_full(h, v) for v, h in zip(inverses, halves)]
        size *= 2
    corner = -dot_full(dot_full(inverses[0], strict[:HALF, HALF:]), inverses[1])
    top = jnp.concatenate([inverses[0], corner], axis=1) / d_row
    return jnp.concatenate([top, inverses[1] / d_row[:, HALF:]], axis=1)


def unpack_tri(packed):
    low = jnp.concatenate([jnp.zeros((HALF, HALF), F32), packed[:, BLK:]], axis=1)
    return jnp.concatenate([packed[:, :BLK], low], axis=0)


def gather_kernel(
    train, scales_hbm, tests_hbm, panel, acc, a0, w0,
    tests, scales, pv, tv, th, tile, slots, group, gathered, feat_t, feat_s, feat_h, a1, w1, p0, p1, p0f,
    vsrc, usrc, gv, gu,
    lsem, sa, ra, sb, rb, svy, svz, rv1, suy, suz, ru1, svx, rvx, sux, rux, line_ready,
):
    m = lax.axis_index("rows")
    x = lax.axis_index("cols")
    z, y, c = m // 8, (m // 2) % NY, m % 2
    q = m % 8
    is_src = m < 2
    xc = x * 2 + c

    def at(zz, yy, cc, xx):
        return ((zz % NZ) * 8 + (yy % NY) * 2 + cc % 2, xx % NX)

    def in_group(k):
        return (z * 8 + (q + k) % 8, x)

    def in_line(k):
        return at(z + k, y, c, x)

    def in_cross(k):
        o = (xc + k) % 8
        return (z * 8 + y * 2 + o % 2, o // 2)

    loads = [
        pltpu.make_async_copy(panel.at[0], pv.at[0], lsem.at[0]),
        pltpu.make_async_copy(train.at[:, :, pl.ds(pl.multiple_of(m * BLK, BLK), BLK)], tv, lsem.at[1]),
        pltpu.make_async_copy(train.at[:, :, pl.ds(0, 2 * BLK)], th, lsem.at[2]),
        pltpu.make_async_copy(panel.at[pl.ds(1, 3)], pv.at[pl.ds(1, 3)], lsem.at[3]),
        pltpu.make_async_copy(scales_hbm, scales, lsem.at[4]),
    ]
    load_tests = pltpu.make_async_copy(tests_hbm, tests, lsem.at[5])
    load_tests.start()
    for copy in loads:
        copy.start()

    barrier = pltpu.get_barrier_semaphore()
    is_deputy = (m == 2) | (m == 3)
    for k in range(1, 8):
        line = (z + k) % NZ
        deputy = jnp.where((line == 0) & (y == 0), 1, y)
        for who in (in_group(k), in_cross(k), at(line, deputy, c, x)):
            pl.semaphore_signal(barrier, inc=1, device_id=who, device_id_type=MESH)

    tile[...] = jnp.zeros((DIM, 128), F32)
    load_tests.wait()
    tile[:, pl.ds(0, 32)] = tests[:, 0, :]

    my_rows = pl.ds(pl.multiple_of(x * PIECE, PIECE), PIECE)
    loads[0].wait()

    @pl.when(is_src)
    def _():
        vsrc[...] = upper_inverse(pv[0, pl.ds(pl.multiple_of(c * BLK, BLK), BLK), :])
        usrc[...] = jnp.concatenate([pv[0, pl.ds(0, HALF), :], pv[0, pl.ds(HALF, HALF), :]], axis=1)

    pl.semaphore_wait(barrier, jnp.where(is_src, 14, jnp.where(is_deputy, 28, 21)))

    @pl.when(is_deputy)
    def _():
        pl.semaphore_signal(line_ready, inc=1, device_id=(c, x), device_id_type=MESH)

    def remote(src, dst, ssem, rsem, who):
        return pltpu.make_async_remote_copy(
            src_ref=src, dst_ref=dst, send_sem=ssem, recv_sem=rsem, device_id=who, device_id_type=MESH
        )

    def send_a(k):
        return remote(tile, slots.at[q], sa.at[k], ra.at[q], in_group(k))

    def send_b(k):
        return remote(group, gathered.at[z], sb.at[k], rb.at[z], in_line(k))

    def send_vy(k):
        return remote(vsrc.at[my_rows], gv.at[c, my_rows], svy.at[k], rv1, at(0, k, c, x))

    def send_uy(k):
        return remote(usrc.at[my_rows], gu.at[my_rows], suy.at[k], ru1, at(0, k, c, x))

    def send_vz(k):
        return remote(gv.at[c, my_rows], gv.at[c, my_rows], svz.at[k], rv1, at(k, y, c, x))

    def send_uz(k):
        return remote(gu.at[my_rows], gu.at[my_rows], suz.at[k], ru1, at(k, y, c, x))

    def send_vx(k):
        return remote(gv.at[c, my_rows], gv.at[c, my_rows], svx.at[k], rvx.at[c, x], in_cross(k))

    def send_ux(k):
        return remote(gu.at[my_rows], gu.at[my_rows], sux.at[k], rux.at[x], in_cross(k))

    def start(send, count):
        for k in range(1, count):
            send(k).start()

    not_src = jnp.logical_not(is_src)
    start(send_a, 8)

    @pl.when(is_src)
    def _():
        start(send_vy, NY)
        gv[c, my_rows, :] = vsrc[my_rows, :]

    @pl.when(is_src & (c == 1))
    def _():
        start(send_uy, NY)
        gu[my_rows, :] = usrc[my_rows, :]

    @pl.when(is_src)
    def _():
        pl.semaphore_wait(line_ready, 1)

    @pl.when((z == 0) & (c == 1) & not_src)
    def _():
        send_vy(1).wait_recv()

    @pl.when((z == 0) & (c == 1))
    def _():
        start(send_vz, NZ)
        start(send_vx, 8)

    @pl.when((z == 0) & (c == 1) & not_src)
    def _():
        send_uy(1).wait_recv()

    @pl.when((z == 0) & (c == 1))
    def _():
        start(send_uz, NZ)
        start(send_ux, 8)

    slots[q] = tile[...]
    for k in range(1, 8):
        o = (q + k) % 8
        remote(tile, slots.at[o], sa.at[k], ra.at[o], in_group(k)).wait_recv()
    for h in range(2):
        total = slots[4 * h]
        for j in range(1, 4):
            total = total + pltpu.roll(slots[4 * h + j], 32 * j, 1)
        group[:, pl.ds(128 * h, 128)] = total

    start(send_b, 8)
    gathered[z] = group[...]

    @pl.when((z == 0) & (c == 0) & not_src)
    def _():
        send_vy(1).wait_recv()

    @pl.when((z == 0) & (c == 0))
    def _():
        start(send_vz, NZ)
        start(send_vx, 8)

    for copy in loads[1:]:
        copy.wait()
    row8 = lax.broadcasted_iota(jnp.int32, (DIM, 1), 0)
    scale = jnp.zeros((DIM, 1), F32)
    for d in range(DIM):
        scale = jnp.where(row8 == d, scales[d], scale)

    feat_h[...] = features(th[:, 0, :] / scale, LOG2E, True).astype(BF16)
    eye = jnp.where(
        lax.broadcasted_iota(jnp.int32, (BLK, BLK), 0) == lax.broadcasted_iota(jnp.int32, (BLK, BLK), 1), -1.0, 0.0
    )
    for r in range(ROUNDS):
        cols = pl.ds(r * BLK, BLK)
        feat_s[:, cols] = features(tv[:, r, :] / scale, LOG2E, True).astype(BF16)
        lower = pv[r, pl.ds(0, BLK), :]
        upper = pv[r, pl.ds(BLK, BLK), :]
        if r == 0:
            lower = jnp.where(is_src, jnp.where(c == 0, eye, 0.0), lower)
            upper = jnp.where(is_src, jnp.where(c == 1, eye, 0.0), upper)
        p0f[:, cols] = lower
        h, l = parts2(upper)
        p1[pl.ds(0, BLK), cols] = h
        p1[pl.ds(BLK, BLK), cols] = h
        p1[pl.ds(2 * BLK, BLK), cols] = l

    def wait_v(cc):
        for k in range(NX):
            rows = pl.ds(k * PIECE, PIECE)

            @pl.when(jnp.logical_or(x != k, c != cc))
            def _():
                remote(gv.at[cc, rows], gv.at[cc, rows], svx.at[0], rvx.at[cc, k], in_cross(1)).wait_recv()

    def wait_u():
        for k in range(NX):
            rows = pl.ds(k * PIECE, PIECE)

            @pl.when(jnp.logical_or(x != k, c != 1))
            def _():
                remote(gu.at[rows], gu.at[rows], sux.at[0], rux.at[k], in_cross(1)).wait_recv()

    def stack(ref, value):
        h, l = parts2(value)
        ref[pl.ds(0, BLK), :] = h
        ref[pl.ds(BLK, BLK), :] = h
        ref[pl.ds(2 * BLK, BLK), :] = l

    def first_weights():
        wait_v(1)
        stack(w1, dot(wide(unpack_tri(gv[1])), p1[...]))

    def second_weights():
        wait_u()
        u01 = jnp.concatenate([gu[:, :BLK], gu[:, BLK:]], axis=0)
        stack(p0, p0f[...] - dot(wide(u01), w1[...]))
        wait_v(0)
        stack(w0, dot(wide(unpack_tri(gv[0])), p0[...]))

    keep = jnp.where(is_src, 0.0, 1.0)

    def covariance(half):
        for slot in range(half * NZ // 2, (half + 1) * NZ // 2):
            o = (z + ARRIVAL[slot]) % NZ
            if slot:
                remote(group, gathered.at[o], sb.at[0], rb.at[o], in_line(1)).wait_recv()
            feat_t[pl.ds(slot * CHUNK, CHUNK), :] = features(gathered[o] / scale, 1.0, False).T.astype(BF16)
        rows = pl.ds(half * TALL, TALL)
        block = jnp.exp2(dot(feat_t[rows, :], feat_h[...]))
        a0[rows, :] = wide(block[:, :BLK])
        a1[rows, :] = wide(block[:, BLK:])
        block = jnp.exp2(dot(feat_t[rows, :], feat_s[...]))
        acc[rows, pl.ds(0, BLK)] = block[:, :BLK] * keep
        acc[rows, pl.ds(BLK, COLS - BLK)] = block[:, BLK:]

    @pl.when((z > 0) & (c == 1))
    def _():
        send_vy(1).wait_recv()
        start(send_vx, 8)

    @pl.when((z > 0) & (c == 1))
    def _():
        send_uy(1).wait_recv()
        start(send_ux, 8)

    @pl.when(z == 0)
    def _():
        first_weights()

    far = (z >= 3) & (z <= 5)
    near = (z > 0) & jnp.logical_not(far)
    covariance(0)

    @pl.when(near & (c == 0))
    def _():
        send_vy(1).wait_recv()
        start(send_vx, 8)


    covariance(1)

    @pl.when(far & (c == 0))
    def _():
        send_vy(1).wait_recv()
        start(send_vx, 8)

    @pl.when(z > 0)
    def _():
        first_weights()

    for i in range(TESTS // TALL):
        rows = pl.ds(i * TALL, TALL)
        acc[rows, :] = acc[rows, :] - dot(a1[rows, :], w1[...])

    second_weights()

    def sent(send, count):
        for k in range(1, count):
            send(k).wait_send()

    for send in (send_a, send_b, send_vx):
        sent(send, 8)

    @pl.when(z == 0)
    def _():
        sent(send_vz, NZ)

    @pl.when(c == 1)
    def _():
        sent(send_ux, 8)

    @pl.when((z == 0) & (c == 1))
    def _():
        sent(send_uz, NZ)

    @pl.when(is_src)
    def _():
        sent(send_vy, NY)

    @pl.when(is_src & (c == 1))
    def _():
        sent(send_uy, NY)


def finish_kernel(acc, a0, w0, out, done, sem):
    z = lax.axis_index("rows") // 8
    copies = []
    first = 0
    for count in SIZES:
        rows = pl.ds(first * CHUNK, count * CHUNK)
        block = acc[rows, :] - dot(a0[rows, :], w0[...])
        for r in range(ROUNDS):
            done[r, rows, :] = block[:, r * BLK:(r + 1) * BLK]
        for i in range(first, first + count):
            tests = pl.ds(pl.multiple_of((z + ARRIVAL[i]) % NZ * CHUNK, CHUNK), CHUNK)
            for r in range(ROUNDS):
                source = done.at[r, pl.ds(i * CHUNK, CHUNK)]
                copies.append(pltpu.make_async_copy(source, out.at[r, tests], sem.at[i * ROUNDS + r]))
                copies[-1].start()
        first += count
    for copy in copies:
        copy.wait()


def per_device(train_points, length_scales, test_points, lower_panel):
    vmem = pl.BlockSpec(memory_space=pltpu.VMEM)
    dma = pltpu.SemaphoreType.DMA
    acc, a0, w0 = pl.pallas_call(
        gather_kernel,
        out_shape=(
            pltpu.VMEM((TESTS, COLS), F32),
            pltpu.VMEM((TESTS, 3 * BLK), BF16),
            pltpu.VMEM((3 * BLK, COLS), BF16),
        ),
        in_specs=[pl.BlockSpec(memory_space=pltpu.HBM)] * 4,
        out_specs=(vmem, vmem, vmem),
        scratch_shapes=[
            pltpu.VMEM((DIM, 1, 32), F32),
            pltpu.SMEM((DIM,), F32),
            pltpu.VMEM((ROUNDS, 2 * BLK, BLK), F32),
            pltpu.VMEM((DIM, ROUNDS, BLK), F32),
            pltpu.VMEM((DIM, ROUNDS, 2 * BLK), F32),
            pltpu.VMEM((DIM, 128), F32),
            pltpu.VMEM((8, DIM, 128), F32),
            pltpu.VMEM((DIM, CHUNK), F32),
            pltpu.VMEM((NZ, DIM, CHUNK), F32),
            pltpu.VMEM((TESTS, FEAT), BF16),
            pltpu.VMEM((FEAT, COLS), BF16),
            pltpu.VMEM((FEAT, 2 * BLK), BF16),
            pltpu.VMEM((TESTS, 3 * BLK), BF16),
            pltpu.VMEM((3 * BLK, COLS), BF16),
            pltpu.VMEM((3 * BLK, COLS), BF16),
            pltpu.VMEM((3 * BLK, COLS), BF16),
            pltpu.VMEM((BLK, COLS), F32),
            pltpu.VMEM((HALF, TRI), F32),
            pltpu.VMEM((HALF, SQ), F32),
            pltpu.VMEM((2, HALF, TRI), F32),
            pltpu.VMEM((HALF, SQ), F32),
            dma((6,)),
            dma((8,)), dma((8,)), dma((8,)), dma((8,)),
            dma((NY,)), dma((NZ,)), dma, dma((NY,)), dma((NZ,)), dma,
            dma((8,)), dma((2, NX)), dma((8,)), dma((NX,)),
            pltpu.SemaphoreType.REGULAR,
        ],
        compiler_params=pltpu.CompilerParams(
            collective_id=0, has_side_effects=True, vmem_limit_bytes=32 * 1024 * 1024
        ),
        name="gather_and_half",
    )(*(pltpu.with_memory_space_constraint(a, pltpu.HBM) for a in (train_points, length_scales, test_points, lower_panel)))
    return pl.pallas_call(
        finish_kernel,
        out_shape=jax.ShapeDtypeStruct((ROUNDS, TESTS, BLK), F32),
        in_specs=[vmem, vmem, vmem],
        out_specs=pl.BlockSpec(memory_space=pltpu.HBM),
        scratch_shapes=[pltpu.VMEM((ROUNDS, TESTS, BLK), F32), dma((ROUNDS * NZ,))],
        compiler_params=pltpu.CompilerParams(vmem_limit_bytes=24 * 1024 * 1024),
        name="finish",
    )(acc, a0, w0)


def solution(mesh):
    placed = (P(), P(), P(None, "cols", "rows"), P(None, None, "rows"))
    return jax.shard_map(
        per_device, mesh=mesh, in_specs=placed, out_specs=P(None, "cols", "rows"), check_vma=False
    )
```

```python
import functools
import math

import jax
import jax.numpy as jnp
from jax import lax
from jax.experimental import pallas as pl
from jax.experimental.pallas import tpu as pltpu
from jax.sharding import PartitionSpec as P

MESH = pl.DeviceIdType.MESH
F32, BF16 = jnp.float32, jnp.bfloat16
LOG2E = math.log2(math.e)

NX, NY, NZ, NC = 4, 4, 8, 2
BLK = 256
HALF = BLK // 2
ROUNDS = 4
DIM = 8
TESTS = 2048
CHUNK = TESTS // NZ
TALL = TESTS // 2
SIZES = (1, 1, 2, 2, 1, 1)
ARRIVAL = (0, 1, 7, 2, 6, 3, 5, 4)
COLS = ROUNDS * BLK
FEAT = 64
PIECE = HALF // NX
STRIP = BLK // NX
TRI = 10 * STRIP
TRI_PIECE = STRIP // NX
SQ = 2 * BLK


def dot(a, b):
    return jnp.dot(a, b, preferred_element_type=F32)


def dot_full(a, b):
    return jnp.dot(a, b, preferred_element_type=F32, precision=lax.Precision.HIGHEST)


def parts3(x):
    h = x.astype(BF16).astype(F32)
    m = (x - h).astype(BF16).astype(F32)
    l = (x - h - m).astype(BF16).astype(F32)
    return h, m, l


def parts2(x):
    h = x.astype(BF16)
    return h, (x - h.astype(F32)).astype(BF16)


def wide(x):
    h, l = parts2(x)
    return jnp.concatenate([h, l, h], axis=1)


def features(points, factor, mirrored):
    n = points.shape[1]
    norm = (-0.5 * LOG2E) * jnp.sum(points * points, axis=0, keepdims=True)
    p1, p2, p3 = parts3(points * factor)
    n1, n2, n3 = parts3(norm)
    row = lax.broadcasted_iota(jnp.int32, (DIM, n), 0)
    base = 3 if mirrored else 0
    own = jnp.where(row == base, n1, jnp.where(row == base + 1, n2, n3))
    mine = (row >= base) & (row < base + 3)
    tail = jnp.where(mine, own, jnp.where(row < 6, 1.0, 0.0))
    order = (p1, p2, p1, p2, p3, p1) if mirrored else (p1, p1, p2, p2, p1, p3)
    return jnp.concatenate(list(order) + [tail, jnp.zeros((DIM, n), F32)], axis=0)


def upper_inverse(u):
    row = lax.broadcasted_iota(jnp.int32, (BLK, BLK), 0)
    col = lax.broadcasted_iota(jnp.int32, (BLK, BLK), 1)
    on_diag = jnp.where(row == col, u, 0.0)
    d_col = jnp.sum(on_diag, axis=1, keepdims=True)
    d_row = jnp.sum(on_diag, axis=0, keepdims=True)
    strict = jnp.where(col > row, u, 0.0) / d_col
    row, col = row[:HALF, :HALF], col[:HALF, :HALF]
    blocks = [strict[:HALF, :HALF], strict[HALF:, HALF:]]
    size = 32
    powers = [jnp.where(row // size == col // size, -n, 0.0) for n in blocks]
    inverses = [jnp.where(row == col, 1.0, 0.0) + p for p in powers]
    for _ in range(4):
        powers = [dot_full(p, p) for p in powers]
        inverses = [v + dot_full(v, p) for v, p in zip(inverses, powers)]
    while size < HALF:
        pair = (row // (2 * size) == col // (2 * size)) & (row // size != col // size)
        halves = [dot_full(v, jnp.where(pair, n, 0.0)) for v, n in zip(inverses, blocks)]
        inverses = [v - dot_full(h, v) for v, h in zip(inverses, halves)]
        size *= 2
    corner = -dot_full(dot_full(inverses[0], strict[:HALF, HALF:]), inverses[1])
    top = jnp.concatenate([inverses[0], corner], axis=1) / d_row
    low = jnp.concatenate([jnp.zeros((HALF, HALF), F32), inverses[1] / d_row[:, HALF:]], axis=1)
    return jnp.concatenate([top, low], axis=0)


def pack_tri(v):
    return jnp.concatenate([v[k * STRIP:(k + 1) * STRIP, k * STRIP:] for k in range(NX)], axis=1)


def unpack_tri(packed):
    strips, first = [packed[:, :BLK]], BLK
    for k in range(1, NX):
        width = BLK - k * STRIP
        strip = packed[:, first:first + width]
        strips.append(jnp.concatenate([jnp.zeros((STRIP, k * STRIP), F32), strip], axis=1))
        first += width
    return jnp.concatenate(strips, axis=0)


def gather_kernel(
    train, scales_hbm, tests_hbm, panel, acc, a0, w0,
    tests, scales, pv, tv, th, tile, slots, group, gathered, feat_t, feat_s, feat_h, a1, w1, p0, p1, p0f,
    vsrc, usrc, gv, gu,
    lsem, sa, ra, sb, rb, svy, svz, rv1, suy, suz, ru1, svx, rvx, sux, rux, line_ready,
):
    m = lax.axis_index("rows")
    x = lax.axis_index("cols")
    z, y, c = m // 8, (m // 2) % NY, m % 2
    q = m % 8
    is_src = m < 2
    xc = x * 2 + c

    def at(zz, yy, cc, xx):
        return ((zz % NZ) * 8 + (yy % NY) * 2 + cc % 2, xx % NX)

    def in_group(k):
        return (z * 8 + (q + k) % 8, x)

    def in_line(k):
        return at(z + k, y, c, x)

    def in_cross(k):
        o = (xc + k) % 8
        return (z * 8 + y * 2 + o % 2, o // 2)

    loads = [
        pltpu.make_async_copy(panel.at[0], pv.at[0], lsem.at[0]),
        pltpu.make_async_copy(train.at[:, :, pl.ds(pl.multiple_of(m * BLK, BLK), BLK)], tv, lsem.at[1]),
        pltpu.make_async_copy(train.at[:, :, pl.ds(0, 2 * BLK)], th, lsem.at[2]),
        pltpu.make_async_copy(panel.at[pl.ds(1, 3)], pv.at[pl.ds(1, 3)], lsem.at[3]),
        pltpu.make_async_copy(scales_hbm, scales, lsem.at[4]),
    ]
    load_tests = pltpu.make_async_copy(tests_hbm, tests, lsem.at[5])
    load_tests.start()
    for copy in loads:
        copy.start()

    barrier = pltpu.get_barrier_semaphore()
    is_deputy = (m == 2) | (m == 3)
    for k in range(1, 8):
        line = (z + k) % NZ
        deputy = jnp.where((line == 0) & (y == 0), 1, y)
        for who in (in_group(k), in_cross(k), at(line, deputy, c, x)):
            pl.semaphore_signal(barrier, inc=1, device_id=who, device_id_type=MESH)

    tile[...] = jnp.zeros((DIM, 128), F32)
    load_tests.wait()
    tile[:, pl.ds(0, 32)] = tests[:, 0, :]

    my_rows = pl.ds(pl.multiple_of(x * PIECE, PIECE), PIECE)
    tri_rows = pl.ds(pl.multiple_of(x * TRI_PIECE, TRI_PIECE), TRI_PIECE)
    loads[0].wait()

    @pl.when(is_src)
    def _():
        vsrc[...] = pack_tri(upper_inverse(pv[0, pl.ds(pl.multiple_of(c * BLK, BLK), BLK), :]))
        usrc[...] = jnp.concatenate([pv[0, pl.ds(0, HALF), :], pv[0, pl.ds(HALF, HALF), :]], axis=1)

    pl.semaphore_wait(barrier, jnp.where(is_src, 14, jnp.where(is_deputy, 28, 21)))

    @pl.when(is_deputy)
    def _():
        pl.semaphore_signal(line_ready, inc=1, device_id=(c, x), device_id_type=MESH)

    def remote(src, dst, ssem, rsem, who):
        return pltpu.make_async_remote_copy(
            src_ref=src, dst_ref=dst, send_sem=ssem, recv_sem=rsem, device_id=who, device_id_type=MESH
        )

    def send_a(k):
        return remote(tile, slots.at[q], sa.at[k], ra.at[q], in_group(k))

    def send_b(k):
        return remote(group, gathered.at[z], sb.at[k], rb.at[z], in_line(k))

    def send_vy(k):
        return remote(vsrc.at[tri_rows], gv.at[c, tri_rows], svy.at[k], rv1, at(0, k, c, x))

    def send_uy(k):
        return remote(usrc.at[my_rows], gu.at[my_rows], suy.at[k], ru1, at(0, k, c, x))

    def send_vz(k):
        return remote(gv.at[c, tri_rows], gv.at[c, tri_rows], svz.at[k], rv1, at(k, y, c, x))

    def send_uz(k):
        return remote(gu.at[my_rows], gu.at[my_rows], suz.at[k], ru1, at(k, y, c, x))

    def send_vx(k):
        return remote(gv.at[c, tri_rows], gv.at[c, tri_rows], svx.at[k], rvx.at[c, x], in_cross(k))

    def send_ux(k):
        return remote(gu.at[my_rows], gu.at[my_rows], sux.at[k], rux.at[x], in_cross(k))

    def start(send, count):
        for k in range(1, count):
            send(k).start()

    not_src = jnp.logical_not(is_src)
    start(send_a, 8)

    @pl.when(is_src)
    def _():
        start(send_vy, NY)
        gv[c, tri_rows, :] = vsrc[tri_rows, :]

    @pl.when(is_src & (c == 1))
    def _():
        start(send_uy, NY)
        gu[my_rows, :] = usrc[my_rows, :]

    @pl.when(is_src)
    def _():
        pl.semaphore_wait(line_ready, 1)

    @pl.when((z == 0) & (c == 1) & not_src)
    def _():
        send_vy(1).wait_recv()

    @pl.when((z == 0) & (c == 1))
    def _():
        start(send_vz, NZ)
        start(send_vx, 8)

    @pl.when((z == 0) & (c == 1) & not_src)
    def _():
        send_uy(1).wait_recv()

    @pl.when((z == 0) & (c == 1))
    def _():
        start(send_uz, NZ)
        start(send_ux, 8)

    slots[q] = tile[...]
    for k in range(1, 8):
        o = (q + k) % 8
        remote(tile, slots.at[o], sa.at[k], ra.at[o], in_group(k)).wait_recv()
    for h in range(2):
        total = slots[4 * h]
        for j in range(1, 4):
            total = total + pltpu.roll(slots[4 * h + j], 32 * j, 1)
        group[:, pl.ds(128 * h, 128)] = total

    start(send_b, 8)
    gathered[z] = group[...]

    @pl.when((z == 0) & (c == 0) & not_src)
    def _():
        send_vy(1).wait_recv()

    @pl.when((z == 0) & (c == 0))
    def _():
        start(send_vz, NZ)
        start(send_vx, 8)

    for copy in loads[1:]:
        copy.wait()
    row8 = lax.broadcasted_iota(jnp.int32, (DIM, 1), 0)
    scale = jnp.zeros((DIM, 1), F32)
    for d in range(DIM):
        scale = jnp.where(row8 == d, scales[d], scale)

    feat_h[...] = features(th[:, 0, :] / scale, LOG2E, True).astype(BF16)
    eye = jnp.where(
        lax.broadcasted_iota(jnp.int32, (BLK, BLK), 0) == lax.broadcasted_iota(jnp.int32, (BLK, BLK), 1), -1.0, 0.0
    )
    for r in range(ROUNDS):
        cols = pl.ds(r * BLK, BLK)
        feat_s[:, cols] = features(tv[:, r, :] / scale, LOG2E, True).astype(BF16)
        lower = pv[r, pl.ds(0, BLK), :]
        upper = pv[r, pl.ds(BLK, BLK), :]
        if r == 0:
            lower = jnp.where(is_src, jnp.where(c == 0, eye, 0.0), lower)
            upper = jnp.where(is_src, jnp.where(c == 1, eye, 0.0), upper)
        p0f[:, cols] = lower
        h, l = parts2(upper)
        p1[pl.ds(0, BLK), cols] = h
        p1[pl.ds(BLK, BLK), cols] = h
        p1[pl.ds(2 * BLK, BLK), cols] = l

    def wait_v(cc):
        for k in range(NX):
            rows = pl.ds(k * TRI_PIECE, TRI_PIECE)

            @pl.when(jnp.logical_or(x != k, c != cc))
            def _():
                remote(gv.at[cc, rows], gv.at[cc, rows], svx.at[0], rvx.at[cc, k], in_cross(1)).wait_recv()

    def wait_u():
        for k in range(NX):
            rows = pl.ds(k * PIECE, PIECE)

            @pl.when(jnp.logical_or(x != k, c != 1))
            def _():
                remote(gu.at[rows], gu.at[rows], sux.at[0], rux.at[k], in_cross(1)).wait_recv()

    def stack(ref, value):
        h, l = parts2(value)
        ref[pl.ds(0, BLK), :] = h
        ref[pl.ds(BLK, BLK), :] = h
        ref[pl.ds(2 * BLK, BLK), :] = l

    def first_weights():
        wait_v(1)
        stack(w1, dot(wide(unpack_tri(gv[1])), p1[...]))

    def second_weights():
        wait_u()
        u01 = jnp.concatenate([gu[:, :BLK], gu[:, BLK:]], axis=0)
        stack(p0, p0f[...] - dot(wide(u01), w1[...]))
        wait_v(0)
        stack(w0, dot(wide(unpack_tri(gv[0])), p0[...]))

    keep = jnp.where(is_src, 0.0, 1.0)

    def covariance(half):
        for slot in range(half * NZ // 2, (half + 1) * NZ // 2):
            o = (z + ARRIVAL[slot]) % NZ
            if slot:
                remote(group, gathered.at[o], sb.at[0], rb.at[o], in_line(1)).wait_recv()
            feat_t[pl.ds(slot * CHUNK, CHUNK), :] = features(gathered[o] / scale, 1.0, False).T.astype(BF16)
        rows = pl.ds(half * TALL, TALL)
        block = jnp.exp2(dot(feat_t[rows, :], feat_h[...]))
        a0[rows, :] = wide(block[:, :BLK])
        a1[rows, :] = wide(block[:, BLK:])
        block = jnp.exp2(dot(feat_t[rows, :], feat_s[...]))
        acc[rows, pl.ds(0, BLK)] = block[:, :BLK] * keep
        acc[rows, pl.ds(BLK, COLS - BLK)] = block[:, BLK:]

    @pl.when((z > 0) & (c == 1))
    def _():
        send_vy(1).wait_recv()
        start(send_vx, 8)

    @pl.when((z > 0) & (c == 1))
    def _():
        send_uy(1).wait_recv()
        start(send_ux, 8)

    @pl.when(z == 0)
    def _():
        first_weights()

    far = (z >= 3) & (z <= 5)
    near = (z > 0) & jnp.logical_not(far)
    covariance(0)

    @pl.when(near & (c == 0))
    def _():
        send_vy(1).wait_recv()
        start(send_vx, 8)


    covariance(1)

    @pl.when(far & (c == 0))
    def _():
        send_vy(1).wait_recv()
        start(send_vx, 8)

    @pl.when(z > 0)
    def _():
        first_weights()

    for i in range(TESTS // TALL):
        rows = pl.ds(i * TALL, TALL)
        acc[rows, :] = acc[rows, :] - dot(a1[rows, :], w1[...])

    second_weights()

    def sent(send, count):
        for k in range(1, count):
            send(k).wait_send()

    for send in (send_a, send_b, send_vx):
        sent(send, 8)

    @pl.when(z == 0)
    def _():
        sent(send_vz, NZ)

    @pl.when(c == 1)
    def _():
        sent(send_ux, 8)

    @pl.when((z == 0) & (c == 1))
    def _():
        sent(send_uz, NZ)

    @pl.when(is_src)
    def _():
        sent(send_vy, NY)

    @pl.when(is_src & (c == 1))
    def _():
        sent(send_uy, NY)


def finish_kernel(acc, a0, w0, out, done, sem):
    z = lax.axis_index("rows") // 8
    copies = []
    first = 0
    for count in SIZES:
        rows = pl.ds(first * CHUNK, count * CHUNK)
        block = acc[rows, :] - dot(a0[rows, :], w0[...])
        for r in range(ROUNDS):
            done[r, rows, :] = block[:, r * BLK:(r + 1) * BLK]
        for i in range(first, first + count):
            tests = pl.ds(pl.multiple_of((z + ARRIVAL[i]) % NZ * CHUNK, CHUNK), CHUNK)
            for r in range(ROUNDS):
                source = done.at[r, pl.ds(i * CHUNK, CHUNK)]
                copies.append(pltpu.make_async_copy(source, out.at[r, tests], sem.at[i * ROUNDS + r]))
                copies[-1].start()
        first += count
    for copy in copies:
        copy.wait()


def per_device(train_points, length_scales, test_points, lower_panel):
    vmem = pl.BlockSpec(memory_space=pltpu.VMEM)
    dma = pltpu.SemaphoreType.DMA
    acc, a0, w0 = pl.pallas_call(
        gather_kernel,
        out_shape=(
            pltpu.VMEM((TESTS, COLS), F32),
            pltpu.VMEM((TESTS, 3 * BLK), BF16),
            pltpu.VMEM((3 * BLK, COLS), BF16),
        ),
        in_specs=[pl.BlockSpec(memory_space=pltpu.HBM)] * 4,
        out_specs=(vmem, vmem, vmem),
        scratch_shapes=[
            pltpu.VMEM((DIM, 1, 32), F32),
            pltpu.SMEM((DIM,), F32),
            pltpu.VMEM((ROUNDS, 2 * BLK, BLK), F32),
            pltpu.VMEM((DIM, ROUNDS, BLK), F32),
            pltpu.VMEM((DIM, ROUNDS, 2 * BLK), F32),
            pltpu.VMEM((DIM, 128), F32),
            pltpu.VMEM((8, DIM, 128), F32),
            pltpu.VMEM((DIM, CHUNK), F32),
            pltpu.VMEM((NZ, DIM, CHUNK), F32),
            pltpu.VMEM((TESTS, FEAT), BF16),
            pltpu.VMEM((FEAT, COLS), BF16),
            pltpu.VMEM((FEAT, 2 * BLK), BF16),
            pltpu.VMEM((TESTS, 3 * BLK), BF16),
            pltpu.VMEM((3 * BLK, COLS), BF16),
            pltpu.VMEM((3 * BLK, COLS), BF16),
            pltpu.VMEM((3 * BLK, COLS), BF16),
            pltpu.VMEM((BLK, COLS), F32),
            pltpu.VMEM((STRIP, TRI), F32),
            pltpu.VMEM((HALF, SQ), F32),
            pltpu.VMEM((2, STRIP, TRI), F32),
            pltpu.VMEM((HALF, SQ), F32),
            dma((6,)),
            dma((8,)), dma((8,)), dma((8,)), dma((8,)),
            dma((NY,)), dma((NZ,)), dma, dma((NY,)), dma((NZ,)), dma,
            dma((8,)), dma((2, NX)), dma((8,)), dma((NX,)),
            pltpu.SemaphoreType.REGULAR,
        ],
        compiler_params=pltpu.CompilerParams(
            collective_id=0, has_side_effects=True, vmem_limit_bytes=32 * 1024 * 1024
        ),
        name="gather_and_half",
    )(*(pltpu.with_memory_space_constraint(a, pltpu.HBM) for a in (train_points, length_scales, test_points, lower_panel)))
    return pl.pallas_call(
        finish_kernel,
        out_shape=jax.ShapeDtypeStruct((ROUNDS, TESTS, BLK), F32),
        in_specs=[vmem, vmem, vmem],
        out_specs=pl.BlockSpec(memory_space=pltpu.HBM),
        scratch_shapes=[pltpu.VMEM((ROUNDS, TESTS, BLK), F32), dma((ROUNDS * NZ,))],
        compiler_params=pltpu.CompilerParams(vmem_limit_bytes=24 * 1024 * 1024),
        name="finish",
    )(acc, a0, w0)


def solution(mesh):
    placed = (P(), P(), P(None, "cols", "rows"), P(None, None, "rows"))
    return jax.shard_map(
        per_device, mesh=mesh, in_specs=placed, out_specs=P(None, "cols", "rows"), check_vma=False
    )
```
